1024 devices in a mesh: row: 64 (over z, x), col: 16 (over y, core).
Axes of the slice: x: 8, y: 8, z: 8, core: 2. Of those that a mesh axis runs over, the one named last changes fastest.
Arguments:
- features: bfloat16 [524288, 256], P(('row', 'col')), may hold values from -6 to 6
- w_self: bfloat16 [256, 256], replicated, may hold values from -0.375 to 0.375
- w_neigh: bfloat16 [256, 256], replicated, may hold values from -0.375 to 0.375
- local_weight: bfloat16 [524288, 512], P(('row', 'col')), as said below
- hub_rows: int32 [1024, 1], P(('row', 'col')), may hold values from 0 to 511
- hub_weight: bfloat16 [524288, 1024], P(('row', 'col')), as said below
- send_rows: int32 [1024, 16, 16], P(('row', 'col')), may hold values from 0 to 511
- send_count: int32 [1024, 16], P(('row', 'col')), may hold values from 1 to 16, as said below
- halo_weight: bfloat16 [524288, 256], P(('row', 'col')), as said below
- grad_out: bfloat16 [524288, 256], P(('row', 'col')), may hold values from -6 to 6
Outputs:
- output: bfloat16 [524288, 256], P(('row', 'col'))
- grad_features: bfloat16 [524288, 256], P(('row', 'col'))
- grad_self: float32 [256, 256], replicated
- grad_neigh: float32 [256, 256], replicated
The draws below stay inside these ranges and needn't reach their ends.
Inputs may be any that keep to these rules, and one draw needn't show every extreme that they name: `local_weight`: A weight is zero where there is no edge and positive where there is one. `hub_weight`: A weight is zero where there is no edge and positive where there is one. `halo_weight`: A weight is zero where there is no edge and positive where there is one. `hub_rows`: rows within the owning part's block. `send_rows`: rows within the sending part's block; only the first send_count of each list are sent. `send_count`: in every group of a row index some part receives 16 rows from every part of its group.
All inputs are finite; a program needn't handle non-finite values.
Results may differ from the reference program's by a relative error of at most 0.0051.
Values may be sent and summed in bfloat16 or wider, within the bound.
No kernel may reach another device: no remote copies, remote signals or barrier semaphores. Data moves between devices by JAX's collectives and lax.ppermute only.
A program may use at most 32 MiB of HBM per device.

```python
import jax
import jax.numpy as jnp
from jax import lax

FEAT = 256
NODE_DEV = 512
HUB_DEV = 1
CAP = 16
NODES = 524288
HUBS = 1024
N_COL = 16
DEVICES = 1024


def edge_parts(key, shape, every):
    keep_key, value_key = jax.random.split(key)
    keep = jax.random.randint(keep_key, shape, 0, every) == 0
    uniform_part = jax.random.uniform(value_key, shape, jnp.float32)
    return (keep, uniform_part)


def edge_values(keep, uniform_part, lowest, highest):
    values = lowest * jnp.exp(uniform_part * jnp.log(highest / lowest))
    return jnp.where(keep, values, 0.0).astype(jnp.bfloat16)


def draw_local_weight(key, part):
    key = jax.random.fold_in(key, 11)
    keep, uniform_part = edge_parts(key, (NODES, NODE_DEV), 16)
    return edge_values(keep, uniform_part, 0.01, 10.0)


def draw_hub_weight(key, part):
    key = jax.random.fold_in(key, 23)
    keep, uniform_part = edge_parts(key, (NODES, HUBS), 32)
    return edge_values(keep, uniform_part, 0.01, 10.0)


def draw_halo_weight(key, part):
    key = jax.random.fold_in(key, 37)
    keep, uniform_part = edge_parts(key, (NODES, N_COL * CAP), 8)
    return edge_values(keep, uniform_part, 0.01, 10.0)


def draw_send_count(key, part):
    key = jax.random.fold_in(key, 53)
    base_key, hot_key = jax.random.split(key)
    base = jax.random.randint(base_key, (DEVICES, N_COL), 1, CAP + 1)
    hot = jax.random.randint(hot_key, (DEVICES // N_COL,), 0, N_COL)
    group = jnp.arange(DEVICES, dtype=jnp.int32) // N_COL
    full = jnp.arange(N_COL, dtype=jnp.int32)[None, :] == hot[group][:, None]
    return jnp.where(full, CAP, base).astype(jnp.int32)


def with_ends(array, key, smallest, high):
    spot = [jax.random.randint(jax.random.fold_in(key, axis), (), 0, length) for axis, length in enumerate(array.shape)]
    main_axis = array.shape.index(max(array.shape))
    next_to = spot[:main_axis] + [(spot[main_axis] + 1) % array.shape[main_axis]] + spot[main_axis + 1:]
    return array.at[tuple(spot)].set(smallest).at[tuple(next_to)].set(high)


def block_levels(key, shape, pieces, smallest, high):
    level = 1.0
    for axis_at, blocks in pieces:
        draws = jax.random.uniform(jax.random.fold_in(jax.random.fold_in(key, 6), axis_at), (blocks,), jnp.float32, smallest / len(pieces), high / len(pieces))
        level = level * jnp.repeat(jnp.exp(draws), shape[axis_at] // blocks).reshape((-1,) + (1,) * (len(shape) - 1 - axis_at))
    return level


def normal_values(own_key, dims, width, bound, cuts=(), kind=jnp.bfloat16):
    drawn = width * jax.random.normal(own_key, dims, jnp.float32)
    if cuts:
        drawn = drawn * block_levels(own_key, dims, cuts, -0.22, 0.18)
    return jnp.clip(drawn, -bound, bound).astype(kind)


def setup_inputs(seed: int = 0) -> dict:
    arg_keys = jax.random.split(jax.random.key(seed), 11)
    return {
        "features": normal_values(arg_keys[0], (NODES, FEAT), 1.0, 6.0, ((0, 1024),)),
        "w_self": normal_values(arg_keys[1], (FEAT, FEAT), FEAT ** -0.5, 0.375),
        "w_neigh": normal_values(arg_keys[2], (FEAT, FEAT), FEAT ** -0.5, 0.375),
        "local_weight": draw_local_weight(jax.random.fold_in(arg_keys[10], 71), 0),
        "hub_rows": with_ends(jax.random.randint(arg_keys[4], (DEVICES, HUB_DEV), 0, NODE_DEV), jax.random.fold_in(arg_keys[4], 1), 0, NODE_DEV - 1).astype(jnp.int32),
        "hub_weight": draw_hub_weight(jax.random.fold_in(arg_keys[10], 71), 0),
        "send_rows": with_ends(jax.random.randint(arg_keys[6], (DEVICES, N_COL, CAP), 0, NODE_DEV), jax.random.fold_in(arg_keys[6], 1), 0, NODE_DEV - 1).astype(jnp.int32),
        "send_count": draw_send_count(jax.random.fold_in(arg_keys[10], 71), 0),
        "halo_weight": draw_halo_weight(jax.random.fold_in(arg_keys[10], 71), 0),
        "grad_out": normal_values(arg_keys[9], (NODES, FEAT), 1.0, 6.0, ((0, 1024),)),
    }


def reference(features, w_self, w_neigh, local_weight, hub_rows, hub_weight, send_rows, send_count, halo_weight, grad_out):
    groups = DEVICES
    blocks = features.reshape(groups, NODE_DEV, FEAT)
    device_ids = jnp.arange(groups, dtype=jnp.int32)
    hub_feat = blocks[device_ids[:, None], hub_rows].reshape(HUBS, FEAT)
    senders = (device_ids // N_COL)[:, None] * N_COL + jnp.arange(N_COL, dtype=jnp.int32)[None, :]
    my_col = (device_ids % N_COL)[:, None]
    src_rows = send_rows[senders, my_col]
    src_count = send_count[senders, my_col]
    live_slots = (jnp.arange(CAP, dtype=jnp.int32)[None, None, :] < src_count[:, :, None]).reshape(groups, N_COL * CAP)
    halo_feat = blocks[senders[:, :, None], src_rows].reshape(groups, N_COL * CAP, FEAT)
    halo_used = jnp.where(live_slots[:, None, :], halo_weight.reshape(groups, NODE_DEV, N_COL * CAP), jnp.zeros((), jnp.bfloat16))
    local_blocks = local_weight.reshape(groups, NODE_DEV, NODE_DEV)
    hub_blocks = hub_weight.reshape(groups, NODE_DEV, HUBS)
    grad_blocks = grad_out.reshape(groups, NODE_DEV, FEAT)

    def one_block(carry, inputs):
        hub_acc, acc_self, acc_neigh = carry
        feat, local_w, hub_w, halo_w, halo_x, grad_o = inputs
        agg_sum = jnp.dot(local_w, feat, preferred_element_type=jnp.float32)
        agg_sum = agg_sum + jnp.dot(hub_w, hub_feat, preferred_element_type=jnp.float32)
        agg_sum = agg_sum + jnp.dot(halo_w, halo_x, preferred_element_type=jnp.float32)
        degree = 1.0 + jnp.sum(local_w.astype(jnp.float32), axis=1) + jnp.sum(hub_w.astype(jnp.float32), axis=1) + jnp.sum(halo_w.astype(jnp.float32), axis=1)
        neigh = (agg_sum / degree[:, None]).astype(jnp.bfloat16)
        preact = jnp.dot(feat, w_self, preferred_element_type=jnp.float32) + jnp.dot(neigh, w_neigh, preferred_element_type=jnp.float32)
        sigmoid_pre = jax.nn.sigmoid(preact)
        output = (preact * sigmoid_pre).astype(jnp.bfloat16)
        grad_pre = (grad_o.astype(jnp.float32) * (sigmoid_pre + preact * sigmoid_pre * (1.0 - sigmoid_pre))).astype(jnp.bfloat16)
        acc_self = acc_self + jnp.dot(feat.T, grad_pre, preferred_element_type=jnp.float32)
        acc_neigh = acc_neigh + jnp.dot(neigh.T, grad_pre, preferred_element_type=jnp.float32)
        grad_agg = (jnp.dot(grad_pre, w_neigh.T, preferred_element_type=jnp.float32) / degree[:, None]).astype(jnp.bfloat16)
        grad_local = jnp.dot(grad_pre, w_self.T, preferred_element_type=jnp.float32) + jnp.dot(local_w.T, grad_agg, preferred_element_type=jnp.float32)
        hub_acc = hub_acc + jnp.dot(hub_w.T, grad_agg, preferred_element_type=jnp.float32)
        halo_back = jnp.dot(halo_w.T, grad_agg, preferred_element_type=jnp.float32)
        return (hub_acc, acc_self, acc_neigh), (output, grad_local, halo_back)

    start = (jnp.zeros((HUBS, FEAT), jnp.float32), jnp.zeros((FEAT, FEAT), jnp.float32), jnp.zeros((FEAT, FEAT), jnp.float32))
    carry, stacked = lax.scan(one_block, start, (blocks, local_blocks, hub_blocks, halo_used, halo_feat, grad_blocks))
    hub_acc, grad_self, grad_neigh = carry
    output, grad_local, halo_back = stacked
    grad_total = grad_local.reshape(NODES, FEAT)
    hub_index = (device_ids[:, None] * NODE_DEV + hub_rows).reshape(-1).astype(jnp.int32)
    grad_total = grad_total.at[hub_index].add(hub_acc)
    halo_index = (senders[:, :, None] * NODE_DEV + src_rows).reshape(-1).astype(jnp.int32)
    grad_total = grad_total.at[halo_index].add(halo_back.reshape(-1, FEAT))
    return output.reshape(NODES, FEAT), grad_total.astype(jnp.bfloat16), grad_self, grad_neigh
```

```python
import jax
import jax.numpy as jnp
from jax import lax
from jax.sharding import PartitionSpec as P

F32 = jnp.float32
BF16 = jnp.bfloat16


def dot(a, b):
    return jnp.dot(a, b, preferred_element_type=F32)


def dot_t(a, b):
    return lax.dot_general(a, b, (((0,), (0,)), ((), ())), preferred_element_type=F32)


def dot_nt(a, b):
    return lax.dot_general(a, b, (((1,), (1,)), ((), ())), preferred_element_type=F32)


def exchange(x, axis):
    return lax.all_to_all(x, axis, split_axis=0, concat_axis=0, tiled=True)


def per_device(
    features,
    w_self,
    w_neigh,
    local_weight,
    hub_rows,
    hub_weight,
    send_rows,
    send_count,
    halo_weight,
    grad_out,
):
    nodes, feat = features.shape
    peers, slots = send_rows.shape[1:]
    groups = lax.axis_size("row")
    hubs = hub_weight.shape[1]
    row_ids = jnp.arange(nodes, dtype=jnp.int32)

    pick = jnp.concatenate(
        [
            send_rows[0],
            jnp.broadcast_to(hub_rows, (peers, 1)),
            jnp.full((peers, 1), -1, jnp.int32),
        ],
        axis=1,
    )
    pick_hot = (pick[:, :, None] == row_ids).astype(BF16).reshape(-1, nodes)
    message = dot(pick_hot, features).astype(BF16).reshape(peers, slots + 2, feat)
    count_slot = (jnp.arange(slots + 2) == slots + 1)[None, :, None]
    message = jnp.where(count_slot, send_count[0].astype(BF16)[:, None, None], message)
    got = exchange(message, "col")
    halo_feat = got[:, :slots].reshape(peers * slots, feat)
    group_hubs = got[:, slots]
    counts = got[:, slots + 1, 0].astype(jnp.int32)
    hub_feat = exchange(
        jnp.broadcast_to(group_hubs[None], (groups, peers, feat)), "row"
    ).reshape(hubs, feat)

    live = (jnp.arange(slots, dtype=jnp.int32)[None, :] < counts[:, None]).reshape(-1)
    halo_used = jnp.where(live[None, :], halo_weight, jnp.zeros((), BF16))
    degree = (
        1.0
        + jnp.sum(local_weight.astype(F32), axis=1)
        + jnp.sum(hub_weight.astype(F32), axis=1)
        + jnp.sum(halo_used.astype(F32), axis=1)
    )[:, None]
    agg_sum = dot(local_weight, features) + dot(halo_used, halo_feat) + dot(hub_weight, hub_feat)
    neigh = (agg_sum / degree).astype(BF16)
    preact = dot(features, w_self) + dot(neigh, w_neigh)
    sig = jax.nn.sigmoid(preact)
    output = (preact * sig).astype(BF16)
    grad_pre = (grad_out.astype(F32) * (sig + preact * sig * (1.0 - sig))).astype(BF16)
    part_self = dot_t(features, grad_pre).astype(BF16)
    part_neigh = dot_t(neigh, grad_pre).astype(BF16)
    grad_agg = (dot_nt(grad_pre, w_neigh) / degree).astype(BF16)
    hub_partial = dot_t(hub_weight, grad_agg).astype(BF16)
    weights = jnp.concatenate([part_self, part_neigh], axis=0).reshape(groups, -1, feat)
    share = weights.shape[1]
    partial = jnp.concatenate([hub_partial.reshape(groups, peers, feat), weights], axis=1)
    row_sum = jnp.sum(exchange(partial, "row").astype(F32), axis=0).astype(BF16)

    grad_local = dot_nt(grad_pre, w_self) + dot_t(local_weight, grad_agg)
    halo_back = dot_t(halo_used, grad_agg).astype(BF16).reshape(peers, slots, feat)
    back = exchange(
        jnp.concatenate(
            [
                halo_back,
                row_sum[:peers, None],
                jnp.broadcast_to(row_sum[None, peers:], (peers, share, feat)),
            ],
            axis=1,
        ),
        "col",
    )
    weight_sum = jnp.sum(back[:, slots + 1 :].astype(F32), axis=0).astype(BF16)
    all_weights = exchange(
        jnp.broadcast_to(weight_sum[None], (groups, share, feat)), "row"
    ).reshape(-1, feat).astype(F32)

    returned = back[:, :slots].reshape(-1, feat)
    send_hot = (send_rows[0].reshape(-1)[:, None] == row_ids).astype(BF16)
    own_hub = jnp.sum(back[:, slots].astype(F32), axis=0)
    grad_total = grad_local + dot_t(send_hot, returned)
    grad_total = grad_total + jnp.where((row_ids == hub_rows[0, 0])[:, None], own_hub, 0.0)
    return (
        output,
        grad_total.astype(BF16),
        all_weights[:feat],
        all_weights[feat:],
    )


def solution(mesh):
    rows = P(("row", "col"), None)
    in_specs = (
        rows,
        P(),
        P(),
        rows,
        rows,
        rows,
        P(("row", "col"), None, None),
        rows,
        rows,
        rows,
    )
    return jax.shard_map(
        per_device, mesh=mesh, in_specs=in_specs, out_specs=(rows, rows, P(), P()), check_vma=False
    )
```

```python
import jax
import jax.numpy as jnp
from jax import lax
from jax.sharding import PartitionSpec as P

F32 = jnp.float32
BF16 = jnp.bfloat16


def dot(a, b):
    return jnp.dot(a, b, preferred_element_type=F32)


def dot_t(a, b):
    return lax.dot_general(a, b, (((0,), (0,)), ((), ())), preferred_element_type=F32)


def dot_nt(a, b):
    return lax.dot_general(a, b, (((1,), (1,)), ((), ())), preferred_element_type=F32)


def exchange(x, axis):
    return lax.all_to_all(x, axis, split_axis=0, concat_axis=0, tiled=True)


def per_device(
    features,
    w_self,
    w_neigh,
    local_weight,
    hub_rows,
    hub_weight,
    send_rows,
    send_count,
    halo_weight,
    grad_out,
):
    nodes, feat = features.shape
    peers, slots = send_rows.shape[1:]
    groups = lax.axis_size("row")
    hubs = hub_weight.shape[1]
    row_ids = jnp.arange(nodes, dtype=jnp.int32)

    pick = jnp.concatenate(
        [
            send_rows[0],
            jnp.broadcast_to(hub_rows, (peers, 1)),
            jnp.full((peers, 1), -1, jnp.int32),
        ],
        axis=1,
    )
    pick_hot = (pick[:, :, None] == row_ids).astype(BF16).reshape(-1, nodes)
    message = dot(pick_hot, features).astype(BF16).reshape(peers, slots + 2, feat)
    count_slot = (jnp.arange(slots + 2) == slots + 1)[None, :, None]
    message = jnp.where(count_slot, send_count[0].astype(BF16)[:, None, None], message)
    got = exchange(message, "col")
    halo_feat = got[:, :slots].reshape(peers * slots, feat)
    group_hubs = got[:, slots]
    counts = got[:, slots + 1, 0].astype(jnp.int32)
    half, cols = peers // 2, feat // 2
    core = lax.axis_index("col") % 2
    swap = [(i, i ^ 1) for i in range(peers)]
    half_hubs = jnp.where(core == 0, group_hubs[:half], group_hubs[half:])
    held = exchange(jnp.broadcast_to(half_hubs[None], (groups, half, feat)), "row")
    other = lax.ppermute(held, "col", swap)
    hub_feat = jnp.concatenate(
        [jnp.where(core == 0, held, other), jnp.where(core == 0, other, held)], axis=1
    ).reshape(hubs, feat)

    live = (jnp.arange(slots, dtype=jnp.int32)[None, :] < counts[:, None]).reshape(-1)
    halo_used = jnp.where(live[None, :], halo_weight, jnp.zeros((), BF16))
    degree = (
        1.0
        + jnp.sum(local_weight.astype(F32), axis=1)
        + jnp.sum(hub_weight.astype(F32), axis=1)
        + jnp.sum(halo_used.astype(F32), axis=1)
    )[:, None]
    agg_sum = dot(local_weight, features) + dot(halo_used, halo_feat) + dot(hub_weight, hub_feat)
    neigh = (agg_sum / degree).astype(BF16)
    preact = dot(features, w_self) + dot(neigh, w_neigh)
    sig = jax.nn.sigmoid(preact)
    output = (preact * sig).astype(BF16)
    grad_pre = (grad_out.astype(F32) * (sig + preact * sig * (1.0 - sig))).astype(BF16)
    part_self = dot_t(features, grad_pre)
    part_neigh = dot_t(neigh, grad_pre)
    grad_agg = (dot_nt(grad_pre, w_neigh) / degree).astype(BF16)
    hub_partial = dot_t(hub_weight, grad_agg)

    hub_halves = hub_partial.reshape(groups, 2, half, feat)
    weights = jnp.concatenate([part_self, part_neigh], axis=0).reshape(groups, -1, feat)
    share = weights.shape[1]

    def piece(which):
        hub = jnp.where(which == 0, hub_halves[:, 0], hub_halves[:, 1])
        weight = jnp.where(which == 0, weights[:, :, :cols], weights[:, :, cols:])
        return jnp.concatenate([hub, weight], axis=2).astype(BF16)

    theirs = lax.ppermute(piece(1 - core), "col", swap)
    paired = (piece(core).astype(F32) + theirs.astype(F32)).astype(BF16)
    row_sum = jnp.sum(exchange(paired, "row").astype(F32), axis=0).astype(BF16)

    grad_local = dot_nt(grad_pre, w_self) + dot_t(local_weight, grad_agg)
    halo_back = dot_t(halo_used, grad_agg).astype(BF16).reshape(peers, slots, feat)
    mine = (jnp.arange(peers) // half == core)[:, None, None]
    own_hubs = jnp.concatenate([row_sum[:, :feat]] * 2, axis=0)[:, None]
    own_hubs = jnp.where(mine, own_hubs, jnp.zeros((), BF16))
    fold = share // 2
    own_weights = jnp.concatenate([row_sum[:fold, feat:], row_sum[fold:, feat:]], axis=1)
    back = exchange(
        jnp.concatenate(
            [halo_back, own_hubs, jnp.broadcast_to(own_weights[None], (peers, fold, feat))],
            axis=1,
        ),
        "col",
    )
    weight_sum = jnp.sum(
        back[:, slots + 1 :].astype(F32).reshape(half, 2, fold, feat), axis=0
    ).astype(BF16)
    weight_sum = jnp.concatenate(
        [
            jnp.concatenate([weight_sum[0, :, :cols], weight_sum[1, :, :cols]], axis=1),
            jnp.concatenate([weight_sum[0, :, cols:], weight_sum[1, :, cols:]], axis=1),
        ],
        axis=0,
    )
    all_weights = exchange(
        jnp.broadcast_to(weight_sum[None], (groups, share, feat)), "row"
    ).reshape(-1, feat).astype(F32)

    returned = back[:, :slots].reshape(-1, feat)
    send_hot = (send_rows[0].reshape(-1)[:, None] == row_ids).astype(BF16)
    own_hub = jnp.sum(back[:, slots].astype(F32), axis=0)
    grad_total = grad_local + dot_t(send_hot, returned)
    grad_total = grad_total + jnp.where((row_ids == hub_rows[0, 0])[:, None], own_hub, 0.0)
    return (
        output,
        grad_total.astype(BF16),
        all_weights[:feat],
        all_weights[feat:],
    )


def solution(mesh):
    rows = P(("row", "col"), None)
    in_specs = (
        rows,
        P(),
        P(),
        rows,
        rows,
        rows,
        P(("row", "col"), None, None),
        rows,
        rows,
        rows,
    )
    return jax.shard_map(
        per_device, mesh=mesh, in_specs=in_specs, out_specs=(rows, rows, P(), P()), check_vma=False
    )
```

```python
import jax
import jax.numpy as jnp
from jax import lax
from jax.experimental import pallas as pl
from jax.experimental.pallas import tpu as pltpu
from jax.sharding import PartitionSpec as P

F32 = jnp.float32
BF16 = jnp.bfloat16


def dot(a, b):
    return jnp.dot(a, b, preferred_element_type=F32)


def dot_t(a, b):
    return lax.dot_general(a, b, (((0,), (0,)), ((), ())), preferred_element_type=F32)


def dot_nt(a, b):
    return lax.dot_general(a, b, (((1,), (1,)), ((), ())), preferred_element_type=F32)


def exchange(x, axis):
    return lax.all_to_all(x, axis, split_axis=0, concat_axis=0, tiled=True)


def pack_kernel(features_ref, rows_ref, hub_ref, count_ref, message_ref):
    nodes, feat = features_ref.shape
    peers, slots = rows_ref.shape[1:]
    listed = rows_ref[0]
    wanted = jnp.concatenate([listed[p : p + 1] for p in range(peers)], axis=1)
    row_ids = lax.broadcasted_iota(jnp.int32, (nodes, peers * slots), 0)
    picked = dot_t((row_ids == wanted).astype(BF16), features_ref[...])
    hub_ids = lax.broadcasted_iota(jnp.int32, (8, nodes), 1)
    hub = dot((hub_ids == hub_ref[0, 0]).astype(BF16), features_ref[...])[:1]
    for p in range(peers):
        count = jnp.full((1, feat), count_ref[0, p].astype(F32))
        rows = picked[p * slots : (p + 1) * slots]
        message_ref[p] = jnp.concatenate([rows, hub, count], axis=0).astype(BF16)


def pack(features, send_rows, hub_rows, send_count):
    feat = features.shape[1]
    peers, slots = send_rows.shape[1:]
    vmem = pl.BlockSpec(memory_space=pltpu.VMEM)
    smem = pl.BlockSpec(memory_space=pltpu.SMEM)
    return pl.pallas_call(
        pack_kernel,
        out_shape=jax.ShapeDtypeStruct((peers, slots + 2, feat), BF16),
        in_specs=[vmem, vmem, smem, smem],
        out_specs=vmem,
    )(features, send_rows, hub_rows, send_count)


def per_device(
    features,
    w_self,
    w_neigh,
    local_weight,
    hub_rows,
    hub_weight,
    send_rows,
    send_count,
    halo_weight,
    grad_out,
):
    nodes, feat = features.shape
    peers, slots = send_rows.shape[1:]
    groups = lax.axis_size("row")
    hubs = hub_weight.shape[1]
    row_ids = jnp.arange(nodes, dtype=jnp.int32)

    message = pack(features, send_rows, hub_rows, send_count)
    got = exchange(message, "col")
    halo_feat = got[:, :slots].reshape(peers * slots, feat)
    group_hubs = got[:, slots]
    counts = got[:, slots + 1, 0].astype(jnp.int32)
    half, cols = peers // 2, feat // 2
    core = lax.axis_index("col") % 2
    swap = [(i, i ^ 1) for i in range(peers)]
    half_hubs = jnp.where(core == 0, group_hubs[:half], group_hubs[half:])
    held = exchange(jnp.broadcast_to(half_hubs[None], (groups, half, feat)), "row")
    other = lax.ppermute(held, "col", swap)
    hub_feat = jnp.concatenate(
        [jnp.where(core == 0, held, other), jnp.where(core == 0, other, held)], axis=1
    ).reshape(hubs, feat)

    live = (jnp.arange(slots, dtype=jnp.int32)[None, :] < counts[:, None]).reshape(-1)
    halo_used = jnp.where(live[None, :], halo_weight, jnp.zeros((), BF16))
    degree = (
        1.0
        + jnp.sum(local_weight.astype(F32), axis=1)
        + jnp.sum(hub_weight.astype(F32), axis=1)
        + jnp.sum(halo_used.astype(F32), axis=1)
    )[:, None]
    agg_sum = dot(local_weight, features) + dot(halo_used, halo_feat) + dot(hub_weight, hub_feat)
    neigh = (agg_sum / degree).astype(BF16)
    preact = lax.dot_general(
        jnp.stack([features, neigh]),
        jnp.stack([w_self, w_neigh]),
        (((0, 2), (0, 1)), ((), ())),
        preferred_element_type=F32,
    )
    sig = jax.nn.sigmoid(preact)
    output = (preact * sig).astype(BF16)
    grad_pre = (grad_out.astype(F32) * (sig + preact * sig * (1.0 - sig))).astype(BF16)
    part_self = dot_t(features, grad_pre)
    part_neigh = dot_t(neigh, grad_pre)
    grad_agg = (dot_nt(grad_pre, w_neigh) / degree).astype(BF16)
    hub_partial = dot_t(hub_weight, grad_agg)

    hub_halves = hub_partial.reshape(groups, 2, half, feat)
    weights = jnp.concatenate([part_self, part_neigh], axis=0).reshape(groups, -1, feat)
    share = weights.shape[1]

    def piece(which):
        hub = jnp.where(which == 0, hub_halves[:, 0], hub_halves[:, 1])
        weight = jnp.where(which == 0, weights[:, :, :cols], weights[:, :, cols:])
        return jnp.concatenate([hub, weight], axis=2).astype(BF16)

    theirs = lax.ppermute(piece(1 - core), "col", swap)
    paired = (piece(core).astype(F32) + theirs.astype(F32)).astype(BF16)
    row_sum = jnp.sum(exchange(paired, "row").astype(F32), axis=0).astype(BF16)

    grad_local = dot_nt(grad_pre, w_self) + dot_t(local_weight, grad_agg)
    halo_back = dot_t(halo_used, grad_agg).astype(BF16).reshape(peers, slots, feat)
    mine = (jnp.arange(peers) // half == core)[:, None, None]
    own_hubs = jnp.concatenate([row_sum[:, :feat]] * 2, axis=0)[:, None]
    own_hubs = jnp.where(mine, own_hubs, jnp.zeros((), BF16))
    fold = share // 2
    own_weights = jnp.concatenate([row_sum[:fold, feat:], row_sum[fold:, feat:]], axis=1)
    back = exchange(
        jnp.concatenate(
            [halo_back, own_hubs, jnp.broadcast_to(own_weights[None], (peers, fold, feat))],
            axis=1,
        ),
        "col",
    )
    weight_sum = jnp.sum(
        back[:, slots + 1 :].astype(F32).reshape(half, 2, fold, feat), axis=0
    ).astype(BF16)
    weight_sum = jnp.concatenate(
        [
            jnp.concatenate([weight_sum[0, :, :cols], weight_sum[1, :, :cols]], axis=1),
            jnp.concatenate([weight_sum[0, :, cols:], weight_sum[1, :, cols:]], axis=1),
        ],
        axis=0,
    )
    all_weights = exchange(
        jnp.broadcast_to(weight_sum[None], (groups, share, feat)), "row"
    ).reshape(-1, feat).astype(F32)

    returned = back[:, :slots].reshape(-1, feat)
    send_hot = (send_rows[0].reshape(-1)[:, None] == row_ids).astype(BF16)
    own_hub = jnp.sum(back[:, slots].astype(F32), axis=0)
    grad_total = grad_local + dot_t(send_hot, returned)
    grad_total = grad_total + jnp.where((row_ids == hub_rows[0, 0])[:, None], own_hub, 0.0)
    return (
        output,
        grad_total.astype(BF16),
        all_weights[:feat],
        all_weights[feat:],
    )


def solution(mesh):
    rows = P(("row", "col"), None)
    in_specs = (
        rows,
        P(),
        P(),
        rows,
        rows,
        rows,
        P(("row", "col"), None, None),
        rows,
        rows,
        rows,
    )
    return jax.shard_map(
        per_device, mesh=mesh, in_specs=in_specs, out_specs=(rows, rows, P(), P()), check_vma=False
    )
```

```python
import jax
import jax.numpy as jnp
from jax import lax
from jax.experimental import pallas as pl
from jax.experimental.pallas import tpu as pltpu
from jax.sharding import PartitionSpec as P

F32 = jnp.float32
BF16 = jnp.bfloat16


def dot(a, b):
    return jnp.dot(a, b, preferred_element_type=F32)


def dot_t(a, b):
    return lax.dot_general(a, b, (((0,), (0,)), ((), ())), preferred_element_type=F32)


def dot_nt(a, b):
    return lax.dot_general(a, b, (((1,), (1,)), ((), ())), preferred_element_type=F32)


def exchange(x, axis):
    return lax.all_to_all(x, axis, split_axis=0, concat_axis=0, tiled=True)


def pack_kernel(features_ref, rows_ref, hub_ref, count_ref, message_ref):
    nodes, feat = features_ref.shape
    peers, slots = rows_ref.shape[1:]
    listed = rows_ref[0]
    wanted = jnp.concatenate([listed[p : p + 1] for p in range(peers)], axis=1)
    row_ids = lax.broadcasted_iota(jnp.int32, (nodes, peers * slots), 0)
    picked = dot_t((row_ids == wanted).astype(BF16), features_ref[...])
    hub_ids = lax.broadcasted_iota(jnp.int32, (8, nodes), 1)
    hub = dot((hub_ids == hub_ref[0, 0]).astype(BF16), features_ref[...])[:1]
    for p in range(peers):
        count = jnp.full((1, feat), count_ref[0, p].astype(F32))
        rows = picked[p * slots : (p + 1) * slots]
        message_ref[p] = jnp.concatenate([rows, hub, count], axis=0).astype(BF16)


def pack(features, send_rows, hub_rows, send_count):
    feat = features.shape[1]
    peers, slots = send_rows.shape[1:]
    vmem = pl.BlockSpec(memory_space=pltpu.VMEM)
    smem = pl.BlockSpec(memory_space=pltpu.SMEM)
    return pl.pallas_call(
        pack_kernel,
        out_shape=jax.ShapeDtypeStruct((peers, slots + 2, feat), BF16),
        in_specs=[vmem, vmem, smem, smem],
        out_specs=vmem,
    )(features, send_rows, hub_rows, send_count)


def per_device(
    features,
    w_self,
    w_neigh,
    local_weight,
    hub_rows,
    hub_weight,
    send_rows,
    send_count,
    halo_weight,
    grad_out,
):
    nodes, feat = features.shape
    peers, slots = send_rows.shape[1:]
    groups = lax.axis_size("row")
    hubs = hub_weight.shape[1]
    row_ids = jnp.arange(nodes, dtype=jnp.int32)

    message = pack(features, send_rows, hub_rows, send_count)
    got = exchange(message, "col")
    halo_feat = got[:, :slots].reshape(peers * slots, feat)
    group_hubs = got[:, slots]
    counts = got[:, slots + 1, 0].astype(jnp.int32)
    half, cols = peers // 2, feat // 2
    core = lax.axis_index("col") % 2
    swap = [(i, i ^ 1) for i in range(peers)]
    half_hubs = jnp.where(core == 0, group_hubs[:half], group_hubs[half:])
    held = exchange(jnp.broadcast_to(half_hubs[None], (groups, half, feat)), "row")
    other = lax.ppermute(held, "col", swap)
    hub_feat = jnp.concatenate(
        [jnp.where(core == 0, held, other), jnp.where(core == 0, other, held)], axis=1
    ).reshape(hubs, feat)

    live = (jnp.arange(slots, dtype=jnp.int32)[None, :] < counts[:, None]).reshape(-1)
    halo_used = jnp.where(live[None, :], halo_weight, jnp.zeros((), BF16))
    w_both, hub_weight_t = lax.optimization_barrier(
        (jnp.stack([w_self, w_neigh]), hub_weight.T)
    )
    degree = (
        1.0
        + jnp.sum(local_weight.astype(F32), axis=1)
        + jnp.sum(hub_weight.astype(F32), axis=1)
        + jnp.sum(halo_used.astype(F32), axis=1)
    )[:, None]
    agg_sum = dot(local_weight, features) + dot(halo_used, halo_feat) + dot(hub_weight, hub_feat)
    neigh = (agg_sum / degree).astype(BF16)
    preact = lax.dot_general(
        jnp.stack([features, neigh]),
        w_both,
        (((0, 2), (0, 1)), ((), ())),
        preferred_element_type=F32,
    )
    sig = jax.nn.sigmoid(preact)
    output = (preact * sig).astype(BF16)
    grad_pre = (grad_out.astype(F32) * (sig + preact * sig * (1.0 - sig))).astype(BF16)
    parts = lax.dot_general(
        jnp.stack([features, neigh]),
        grad_pre,
        (((1,), (0,)), ((), ())),
        preferred_element_type=F32,
    )
    grad_agg = (dot_nt(grad_pre, w_neigh) / degree).astype(BF16)
    hub_partial = dot(hub_weight_t, grad_agg)

    hub_halves = hub_partial.reshape(groups, 2, half, feat)
    weights = parts.reshape(groups, -1, feat)
    share = weights.shape[1]

    def piece(which):
        hub = jnp.where(which == 0, hub_halves[:, 0], hub_halves[:, 1])
        weight = jnp.where(which == 0, weights[:, :, :cols], weights[:, :, cols:])
        return jnp.concatenate([hub, weight], axis=2).astype(BF16)

    theirs = lax.ppermute(piece(1 - core), "col", swap)
    paired = (piece(core).astype(F32) + theirs.astype(F32)).astype(BF16)
    row_sum = jnp.sum(exchange(paired, "row").astype(F32), axis=0).astype(BF16)

    grad_local = dot_nt(grad_pre, w_self) + dot_t(local_weight, grad_agg)
    halo_back = dot_t(halo_used, grad_agg).astype(BF16).reshape(peers, slots, feat)
    mine = (jnp.arange(peers) // half == core)[:, None, None]
    own_hubs = jnp.concatenate([row_sum[:, :feat]] * 2, axis=0)[:, None]
    own_hubs = jnp.where(mine, own_hubs, jnp.zeros((), BF16))
    fold = share // 2
    own_weights = jnp.concatenate([row_sum[:fold, feat:], row_sum[fold:, feat:]], axis=1)
    back = exchange(
        jnp.concatenate(
            [halo_back, own_hubs, jnp.broadcast_to(own_weights[None], (peers, fold, feat))],
            axis=1,
        ),
        "col",
    )
    weight_sum = jnp.sum(
        back[:, slots + 1 :].astype(F32).reshape(half, 2, fold, feat), axis=0
    ).astype(BF16)
    weight_sum = jnp.concatenate(
        [
            jnp.concatenate([weight_sum[0, :, :cols], weight_sum[1, :, :cols]], axis=1),
            jnp.concatenate([weight_sum[0, :, cols:], weight_sum[1, :, cols:]], axis=1),
        ],
        axis=0,
    )
    all_weights = exchange(
        jnp.broadcast_to(weight_sum[None], (groups, share, feat)), "row"
    ).reshape(-1, feat).astype(F32)

    returned = back[:, :slots].reshape(-1, feat)
    send_hot = (send_rows[0].reshape(-1)[:, None] == row_ids).astype(BF16)
    own_hub = jnp.sum(back[:, slots].astype(F32), axis=0)
    grad_total = grad_local + dot_t(send_hot, returned)
    grad_total = grad_total + jnp.where((row_ids == hub_rows[0, 0])[:, None], own_hub, 0.0)
    return (
        output,
        grad_total.astype(BF16),
        all_weights[:feat],
        all_weights[feat:],
    )


def solution(mesh):
    rows = P(("row", "col"), None)
    in_specs = (
        rows,
        P(),
        P(),
        rows,
        rows,
        rows,
        P(("row", "col"), None, None),
        rows,
        rows,
        rows,
    )
    return jax.shard_map(
        per_device, mesh=mesh, in_specs=in_specs, out_specs=(rows, rows, P(), P()), check_vma=False
    )
```

```python
import jax
import jax.numpy as jnp
from jax import lax
from jax.experimental import pallas as pl
from jax.experimental.pallas import tpu as pltpu
from jax.sharding import PartitionSpec as P

F32 = jnp.float32
BF16 = jnp.bfloat16


def dot(a, b):
    return jnp.dot(a, b, preferred_element_type=F32)


def dot_t(a, b):
    return lax.dot_general(a, b, (((0,), (0,)), ((), ())), preferred_element_type=F32)


def dot_nt(a, b):
    return lax.dot_general(a, b, (((1,), (1,)), ((), ())), preferred_element_type=F32)


def exchange(x, axis):
    return lax.all_to_all(x, axis, split_axis=0, concat_axis=0, tiled=True)


def pack_kernel(features_ref, rows_ref, hub_ref, count_ref, message_ref):
    nodes, feat = features_ref.shape
    peers, slots = rows_ref.shape[1:]
    listed = rows_ref[0]
    wanted = jnp.concatenate([listed[p : p + 1] for p in range(peers)], axis=1)
    row_ids = lax.broadcasted_iota(jnp.int32, (nodes, peers * slots), 0)
    picked = dot_t((row_ids == wanted).astype(BF16), features_ref[...])
    hub_ids = lax.broadcasted_iota(jnp.int32, (8, nodes), 1)
    hub = dot((hub_ids == hub_ref[0, 0]).astype(BF16), features_ref[...])[:1]
    for p in range(peers):
        count = jnp.full((1, feat), count_ref[0, p].astype(F32))
        rows = picked[p * slots : (p + 1) * slots]
        message_ref[p] = jnp.concatenate([rows, hub, count], axis=0).astype(BF16)


def pack(features, send_rows, hub_rows, send_count):
    feat = features.shape[1]
    peers, slots = send_rows.shape[1:]
    vmem = pl.BlockSpec(memory_space=pltpu.VMEM)
    smem = pl.BlockSpec(memory_space=pltpu.SMEM)
    return pl.pallas_call(
        pack_kernel,
        out_shape=jax.ShapeDtypeStruct((peers, slots + 2, feat), BF16),
        in_specs=[vmem, vmem, smem, smem],
        out_specs=vmem,
    )(features, send_rows, hub_rows, send_count)


def per_device(
    features,
    w_self,
    w_neigh,
    local_weight,
    hub_rows,
    hub_weight,
    send_rows,
    send_count,
    halo_weight,
    grad_out,
):
    nodes, feat = features.shape
    peers, slots = send_rows.shape[1:]
    groups = lax.axis_size("row")
    hubs = hub_weight.shape[1]
    row_ids = jnp.arange(nodes, dtype=jnp.int32)

    message = pack(features, send_rows, hub_rows, send_count)
    got = exchange(message, "col")
    halo_feat = got[:, :slots].reshape(peers * slots, feat)
    group_hubs = got[:, slots]
    counts = got[:, slots + 1, 0].astype(jnp.int32)
    half, cols = peers // 2, feat // 2
    core = lax.axis_index("col") % 2
    swap = [(i, i ^ 1) for i in range(peers)]
    half_hubs = jnp.where(core == 0, group_hubs[:half], group_hubs[half:])
    held = exchange(jnp.broadcast_to(half_hubs[None], (groups, half, feat)), "row")
    other = lax.ppermute(held, "col", swap)
    hub_feat = jnp.concatenate(
        [jnp.where(core == 0, held, other), jnp.where(core == 0, other, held)], axis=1
    ).reshape(hubs, feat)

    live = (jnp.arange(slots, dtype=jnp.int32)[None, :] < counts[:, None]).reshape(-1)
    halo_used = jnp.where(live[None, :], halo_weight, jnp.zeros((), BF16))
    w_both, hub_weight_t, grad_out_wide = lax.optimization_barrier(
        (jnp.stack([w_self, w_neigh]), hub_weight.T, grad_out.astype(F32))
    )
    degree = (
        1.0
        + jnp.sum(local_weight.astype(F32), axis=1)
        + jnp.sum(hub_weight.astype(F32), axis=1)
        + jnp.sum(halo_used.astype(F32), axis=1)
    )[:, None]
    agg_sum = dot(local_weight, features) + dot(halo_used, halo_feat) + dot(hub_weight, hub_feat)
    neigh = (agg_sum / degree).astype(BF16)
    preact = lax.dot_general(
        jnp.stack([features, neigh]),
        w_both,
        (((0, 2), (0, 1)), ((), ())),
        preferred_element_type=F32,
    )
    sig = jax.nn.sigmoid(preact)
    output = (preact * sig).astype(BF16)
    grad_pre = (grad_out_wide * (sig + preact * sig * (1.0 - sig))).astype(BF16)
    parts = lax.dot_general(
        jnp.stack([features, neigh]),
        grad_pre,
        (((1,), (0,)), ((), ())),
        preferred_element_type=F32,
    )
    grad_agg = (dot_nt(grad_pre, w_neigh) / degree).astype(BF16)
    hub_partial = dot(hub_weight_t, grad_agg)

    hub_halves = hub_partial.reshape(groups, 2, half, feat)
    weights = parts.reshape(groups, -1, feat)
    share = weights.shape[1]

    def piece(which):
        hub = jnp.where(which == 0, hub_halves[:, 0], hub_halves[:, 1])
        weight = jnp.where(which == 0, weights[:, :, :cols], weights[:, :, cols:])
        return jnp.concatenate([hub, weight], axis=2).astype(BF16)

    theirs = lax.ppermute(piece(1 - core), "col", swap)
    paired = (piece(core).astype(F32) + theirs.astype(F32)).astype(BF16)
    row_sum = jnp.sum(exchange(paired, "row").astype(F32), axis=0).astype(BF16)

    grad_local = dot_nt(grad_pre, w_self) + dot_t(local_weight, grad_agg)
    halo_back = dot_t(halo_used, grad_agg).astype(BF16).reshape(peers, slots, feat)
    mine = (jnp.arange(peers) // half == core)[:, None, None]
    own_hubs = jnp.concatenate([row_sum[:, :feat]] * 2, axis=0)[:, None]
    own_hubs = jnp.where(mine, own_hubs, jnp.zeros((), BF16))
    fold = share // 2
    own_weights = jnp.concatenate([row_sum[:fold, feat:], row_sum[fold:, feat:]], axis=1)
    back = exchange(
        jnp.concatenate(
            [halo_back, own_hubs, jnp.broadcast_to(own_weights[None], (peers, fold, feat))],
            axis=1,
        ),
        "col",
    )
    weight_sum = jnp.sum(
        back[:, slots + 1 :].astype(F32).reshape(half, 2, fold, feat), axis=0
    ).astype(BF16)
    weight_sum = jnp.concatenate(
        [
            jnp.concatenate([weight_sum[0, :, :cols], weight_sum[1, :, :cols]], axis=1),
            jnp.concatenate([weight_sum[0, :, cols:], weight_sum[1, :, cols:]], axis=1),
        ],
        axis=0,
    )
    all_weights = exchange(
        jnp.broadcast_to(weight_sum[None], (groups, share, feat)), "row"
    ).reshape(-1, feat).astype(F32)

    returned = back[:, :slots].reshape(-1, feat)
    send_hot = (send_rows[0].reshape(-1)[:, None] == row_ids).astype(BF16)
    own_hub = jnp.sum(back[:, slots].astype(F32), axis=0)
    grad_total = grad_local + dot_t(send_hot, returned)
    grad_total = grad_total + jnp.where((row_ids == hub_rows[0, 0])[:, None], own_hub, 0.0)
    return (
        output,
        grad_total.astype(BF16),
        all_weights[:feat],
        all_weights[feat:],
    )


def solution(mesh):
    rows = P(("row", "col"), None)
    in_specs = (
        rows,
        P(),
        P(),
        rows,
        rows,
        rows,
        P(("row", "col"), None, None),
        rows,
        rows,
        rows,
    )
    return jax.shard_map(
        per_device, mesh=mesh, in_specs=in_specs, out_specs=(rows, rows, P(), P()), check_vma=False
    )
```
